512 devices in a mesh: dp: 32 (over z, x_lo, core), head: 16 (over x_hi, y).
Axes of the slice: x: 4 (x_hi: 2, x_lo: 2; x = x_hi * 2 + x_lo), y: 8, z: 8, core: 2. Of those that a mesh axis runs over, the one named last changes fastest.
Arguments:
- stream: bfloat16 [128, 8192], P('head', 'dp'), may hold values from -32.7 to 32.7
- state: float32 [128, 128, 8192], P('dp', 'head'), may hold values from -6 to 6
- mixer_norm_gain: bfloat16 [8192], P('dp'), may hold values from 0.5 to 1.5
- head_input_weight: bfloat16 [8192, 8192], P('dp', 'head'), may hold values from -0.0625 to 0.0625
- output_gate_weight: bfloat16 [8192, 8192], P('dp', 'head'), may hold values from -0.0625 to 0.0625
- group_map_weight: bfloat16 [8192, 2048], P('dp', 'head'), may hold values from -0.0625 to 0.0625
- step_size_weight: bfloat16 [8192, 128], P('dp', 'head'), may hold values from -0.0625 to 0.0625
- step_size_bias: float32 [128], P('head'), may hold values from -3 to 0.5
- head_decay_rate: float32 [128], P('head'), may hold values from 0.5 to 16
- head_skip_gain: float32 [128], P('head'), may hold values from 0.5 to 2
- gate_norm_gain: bfloat16 [8192], P('head'), may hold values from 0.5 to 1.5
- mixer_output_weight: bfloat16 [8192, 8192], P('head', 'dp'), may hold values from -0.0625 to 0.0625
- adapter_input_down: bfloat16 [8, 8192, 16], P(None, 'dp'), may hold values from -0.0625 to 0.0625
- adapter_input_up: bfloat16 [8, 16, 2, 8192], P(None, None, None, 'head'), may hold values from -1.5 to 1.5
- adapter_output_down: bfloat16 [8, 8192, 16], P(None, 'head'), may hold values from -0.0625 to 0.0625
- adapter_output_up: bfloat16 [8, 16, 8192], P(None, None, 'dp'), may hold values from -1.5 to 1.5
- mlp_norm_gain: bfloat16 [8192], P('dp'), may hold values from 0.5 to 1.5
- mlp_up_weight: bfloat16 [8192, 16384], P('dp', 'head'), may hold values from -0.0625 to 0.0625
- mlp_down_weight: bfloat16 [16384, 8192], P('head', 'dp'), may hold values from -0.046875 to 0.046875
- slot_adapter_index: int32 [128], P('dp'), may hold values from 0 to 8, as said below
- segment_first_slot: int32 [8], replicated, may hold values from 0 to 124, as said below
Outputs:
- out_stream: bfloat16 [128, 8192], P('head', 'dp')
- new_state: float32 [128, 128, 8192], P('dp', 'head')
The draws below stay inside these ranges and needn't reach their ends.
Inputs may be any that keep to these rules, and one draw needn't show every extreme that they name: `slot_adapter_index`: row slots form 8 segments, one for each adapter in order of adapter number; each is one or more whole tiles of 4 slots, the last segment exactly one tile; its live rows come first and carry its adapter number, the rest carry 8; each segment has at least one live row and at least one padding slot. `segment_first_slot`: the first slot of each segment described with slot_adapter_index: strictly increasing multiples of 4, the first 0, the last 124.
All inputs are finite; a program needn't handle non-finite values.
Results may differ from the reference program's by a relative error of at most 0.033.
Values may be sent and summed in bfloat16 or wider, within the bound.
No kernel may reach another device: no remote copies, remote signals or barrier semaphores. Data moves between devices by JAX's collectives and lax.ppermute only.
A program may use at most 64 MiB of HBM per device.

```python
import math
import jax
import jax.numpy as jnp
from jax import lax

MODEL_WIDTH = 8192
HEAD_TOTAL = 128
HEAD_CHANNELS = 64
NSTATE = 128
GROUPS = 8
FF = 16384
ADAPTER_RANK = 16
ADAPTER_COUNT = 8
TILE = 4
ROWS = 128
N_DP = 32
N_HEAD = 16


def segment_plan(key):
    tiles_all = ROWS // TILE
    cut_key, live_key = jax.random.split(key)
    shuffled = jax.random.permutation(cut_key, tiles_all - 2).astype(jnp.int32) + 1
    cuts = jnp.sort(jnp.concatenate([shuffled[:ADAPTER_COUNT - 2], jnp.full((1,), tiles_all - 1, jnp.int32)]))
    bounds = jnp.concatenate([jnp.zeros((1,), jnp.int32), cuts, jnp.full((1,), tiles_all, jnp.int32)])
    tiles_per = bounds[1:] - bounds[:-1]
    last_live = jax.random.randint(live_key, (ADAPTER_COUNT,), 1, TILE).astype(jnp.int32)
    starts = bounds[:-1] * TILE
    live_count = (tiles_per - 1) * TILE + last_live
    return (starts, live_count)


def draw_segment_first_slot(key, part):
    starts, live_count = segment_plan(key)
    return starts.astype(jnp.int32)


def draw_slot_adapter_index(key, part):
    starts, live_count = segment_plan(key)
    slots = jnp.arange(ROWS, dtype=jnp.int32)
    segment = jnp.sum((starts[None, :] <= slots[:, None]).astype(jnp.int32), axis=1) - 1
    position = slots - starts[segment]
    return jnp.where(position < live_count[segment], segment, ADAPTER_COUNT).astype(jnp.int32)


def draw_stream(key, part):
    key = jax.random.fold_in(key, 7)
    row_key, col_key, base_key = jax.random.split(key, 3)
    row_scale = jnp.exp(jax.random.uniform(row_key, (ROWS, 1), jnp.float32, -0.7, 0.7))
    position = jnp.arange(MODEL_WIDTH, dtype=jnp.float32)[None, :] / (MODEL_WIDTH - 1) * 2.0 - 1.0
    trend = 0.6
    col_scale = jnp.exp(jax.random.uniform(col_key, (1, MODEL_WIDTH), jnp.float32, -0.5, 0.5) + trend * position)
    base = jax.random.normal(base_key, (ROWS, MODEL_WIDTH), jnp.float32)
    base = jnp.clip(base, -4.0, 4.0)
    return (base * row_scale * col_scale).astype(jnp.bfloat16)


def block_levels(own_key, dims, cuts, smallest, top_value):
    def one(dim, blocks):
        steps = jax.random.uniform(jax.random.fold_in(jax.random.fold_in(own_key, 6), dim), (blocks,), jnp.float32, smallest / len(cuts), top_value / len(cuts))
        return jnp.repeat(jnp.exp(steps), dims[dim] // blocks).reshape((-1,) + (1,) * (len(dims) - dim - 1))

    level = one(*cuts[0])
    for cut in cuts[1:]:
        level = level * one(*cut)
    return level


def normal_values(key, shape, width, reach, cuts=(), kind=jnp.bfloat16):
    array = width * jax.random.normal(key, shape, jnp.float32)
    if cuts:
        array = array * block_levels(key, shape, cuts, -0.22, 0.18)
    return jnp.clip(array, -reach, reach).astype(kind)


def setup_inputs(seed: int = 0) -> dict:
    key_of = jax.random.split(jax.random.key(seed), 22)
    stream = draw_stream(jax.random.fold_in(key_of[21], 71), 0)
    state = normal_values(key_of[1], (ROWS, HEAD_TOTAL, HEAD_CHANNELS * NSTATE), 1.0, 6.0, ((0, 32), (1, 16)), jnp.float32)
    mixer_norm_gain = jnp.clip(1.0 + 0.1 * jax.random.normal(key_of[2], (MODEL_WIDTH,), jnp.float32), 0.5, 1.5).astype(jnp.bfloat16)
    head_input_weight = normal_values(key_of[3], (MODEL_WIDTH, HEAD_TOTAL * HEAD_CHANNELS), MODEL_WIDTH ** -0.5, 0.0625, ((0, 32), (1, 16)))
    output_gate_weight = normal_values(key_of[4], (MODEL_WIDTH, HEAD_TOTAL * HEAD_CHANNELS), MODEL_WIDTH ** -0.5, 0.0625, ((0, 32), (1, 16)))
    group_map_weight = normal_values(key_of[5], (MODEL_WIDTH, 2 * GROUPS * NSTATE), MODEL_WIDTH ** -0.5, 0.0625, ((0, 32), (1, 16)))
    step_size_weight = normal_values(key_of[6], (MODEL_WIDTH, HEAD_TOTAL), MODEL_WIDTH ** -0.5, 0.0625, ((0, 32), (1, 16)))
    step_size_bias = jnp.clip(-3.0 + 3.5 * jax.random.uniform(key_of[7], (HEAD_TOTAL,), jnp.float32) ** block_levels(key_of[7], (HEAD_TOTAL,), ((0, 16),), -0.2, 0.2), -3.0, 0.5)
    head_decay_rate = jnp.clip(jnp.exp(math.log(16.0) - 3.465736 * jax.random.uniform(key_of[8], (HEAD_TOTAL,), jnp.float32) ** block_levels(key_of[8], (HEAD_TOTAL,), ((0, 16),), -0.2, 0.2)), 0.5, 16.0)
    head_skip_gain = jnp.clip(0.5 + 1.5 * jax.random.uniform(key_of[9], (HEAD_TOTAL,), jnp.float32) ** block_levels(key_of[9], (HEAD_TOTAL,), ((0, 16),), -0.2, 0.2), 0.5, 2.0)
    gate_norm_gain = jnp.clip(1.0 + 0.1 * jax.random.normal(key_of[10], (HEAD_TOTAL * HEAD_CHANNELS,), jnp.float32), 0.5, 1.5).astype(jnp.bfloat16)
    mixer_output_weight = normal_values(key_of[11], (HEAD_TOTAL * HEAD_CHANNELS, MODEL_WIDTH), (HEAD_TOTAL * HEAD_CHANNELS) ** -0.5, 0.0625, ((0, 16), (1, 32)))
    adapter_input_down = normal_values(key_of[12], (ADAPTER_COUNT, MODEL_WIDTH, ADAPTER_RANK), MODEL_WIDTH ** -0.5, 0.0625, ((1, 32),))
    adapter_input_up = normal_values(key_of[13], (ADAPTER_COUNT, ADAPTER_RANK, 2, HEAD_TOTAL * HEAD_CHANNELS), ADAPTER_RANK ** -0.5, 1.5, ((3, 16),))
    adapter_output_down = normal_values(key_of[14], (ADAPTER_COUNT, HEAD_TOTAL * HEAD_CHANNELS, ADAPTER_RANK), (HEAD_TOTAL * HEAD_CHANNELS) ** -0.5, 0.0625, ((1, 16),))
    adapter_output_up = normal_values(key_of[15], (ADAPTER_COUNT, ADAPTER_RANK, MODEL_WIDTH), ADAPTER_RANK ** -0.5, 1.5, ((2, 32),))
    mlp_norm_gain = jnp.clip(1.0 + 0.1 * jax.random.normal(key_of[16], (MODEL_WIDTH,), jnp.float32), 0.5, 1.5).astype(jnp.bfloat16)
    mlp_up_weight = normal_values(key_of[17], (MODEL_WIDTH, FF), MODEL_WIDTH ** -0.5, 0.0625, ((0, 32), (1, 16)))
    mlp_down_weight = normal_values(key_of[18], (FF, MODEL_WIDTH), FF ** -0.5, 0.046875, ((0, 16), (1, 32)))
    slot_adapter_index = draw_slot_adapter_index(jax.random.fold_in(key_of[21], 71), 0)
    segment_first_slot = draw_segment_first_slot(jax.random.fold_in(key_of[21], 71), 0)
    return dict(stream=stream, state=state, mixer_norm_gain=mixer_norm_gain, head_input_weight=head_input_weight, output_gate_weight=output_gate_weight, group_map_weight=group_map_weight, step_size_weight=step_size_weight, step_size_bias=step_size_bias, head_decay_rate=head_decay_rate, head_skip_gain=head_skip_gain, gate_norm_gain=gate_norm_gain, mixer_output_weight=mixer_output_weight, adapter_input_down=adapter_input_down, adapter_input_up=adapter_input_up, adapter_output_down=adapter_output_down, adapter_output_up=adapter_output_up, mlp_norm_gain=mlp_norm_gain, mlp_up_weight=mlp_up_weight, mlp_down_weight=mlp_down_weight, slot_adapter_index=slot_adapter_index, segment_first_slot=segment_first_slot)


highest_precision = lax.Precision.HIGHEST
eps = 1e-05

def reference(stream, state, mixer_norm_gain, head_input_weight, output_gate_weight, group_map_weight, step_size_weight, step_size_bias, head_decay_rate, head_skip_gain, gate_norm_gain, mixer_output_weight, adapter_input_down, adapter_input_up, adapter_output_down, adapter_output_up, mlp_norm_gain, mlp_up_weight, mlp_down_weight, slot_adapter_index, segment_first_slot):
    inner_width = HEAD_TOTAL * HEAD_CHANNELS
    lane_groups = ADAPTER_COUNT * ADAPTER_RANK
    stream_wide = stream.astype(jnp.float32)
    mix_scale = lax.rsqrt(lax.optimization_barrier(jnp.mean(stream_wide * stream_wide, axis=1)) + eps)
    normed = (stream_wide * mix_scale[:, None] * mixer_norm_gain.astype(jnp.float32)[None, :]).astype(jnp.bfloat16)
    tile_starts = jnp.arange(ROWS // TILE, dtype=jnp.int32) * TILE
    tile_adapter = lax.optimization_barrier(jnp.sum((segment_first_slot[None, :] <= tile_starts[:, None]).astype(jnp.int32), axis=1)) - 1
    row_adapter = jnp.repeat(tile_adapter, TILE)
    adapter_pick = (row_adapter[:, None] == jnp.arange(ADAPTER_COUNT, dtype=jnp.int32)[None, :]).astype(jnp.float32)
    live_rows = slot_adapter_index < ADAPTER_COUNT
    input_table = jnp.transpose(adapter_input_down, (1, 0, 2)).reshape(MODEL_WIDTH, lane_groups)
    lane_in = jnp.dot(normed, input_table, preferred_element_type=jnp.float32).reshape(ROWS, ADAPTER_COUNT, ADAPTER_RANK)
    low_in = lax.optimization_barrier(jnp.sum(lane_in * adapter_pick[:, :, None], axis=1))
    spread_input = (adapter_pick[:, :, None] * low_in[:, None, :]).reshape(ROWS, lane_groups)
    input_lift = jnp.dot(spread_input, adapter_input_up.astype(jnp.float32).reshape(lane_groups, 2 * inner_width), precision=highest_precision)
    x_part = jnp.dot(normed, head_input_weight, preferred_element_type=jnp.float32) + input_lift[:, :inner_width]
    z_part = jnp.dot(normed, output_gate_weight, preferred_element_type=jnp.float32) + input_lift[:, inner_width:]
    group_part = jnp.dot(normed, group_map_weight, preferred_element_type=jnp.float32)
    step_raw = jnp.dot(normed, step_size_weight, preferred_element_type=jnp.float32)
    step_size = jax.nn.softplus(step_raw + step_size_bias[None, :])
    forget = jnp.exp(-step_size * head_decay_rate[None, :])
    x_heads = jax.nn.silu(x_part).reshape(ROWS, HEAD_TOTAL, HEAD_CHANNELS)
    input_mat = jax.nn.silu(group_part[:, :GROUPS * NSTATE]).reshape(ROWS, GROUPS, NSTATE)
    output_mat = jax.nn.silu(group_part[:, GROUPS * NSTATE:]).reshape(ROWS, GROUPS, NSTATE)
    head_groups = jnp.arange(HEAD_TOTAL, dtype=jnp.int32) // (HEAD_TOTAL // GROUPS)
    head_input = input_mat[:, head_groups, :]
    head_output = output_mat[:, head_groups, :]
    old_state = state.reshape(ROWS, HEAD_TOTAL, HEAD_CHANNELS, NSTATE)
    fresh = forget[:, :, None, None] * old_state + (step_size[:, :, None] * x_heads)[:, :, :, None] * head_input[:, :, None, :]
    new_state = jnp.where(live_rows[:, None, None, None], fresh, old_state).reshape(state.shape)
    read_out = lax.optimization_barrier(jnp.sum(fresh * head_output[:, :, None, :], axis=3)) + head_skip_gain[None, :, None] * x_heads
    gated = read_out.reshape(ROWS, inner_width) * jax.nn.silu(z_part)
    grouped = gated.reshape(ROWS, GROUPS, inner_width // GROUPS)
    group_scale = lax.rsqrt(lax.optimization_barrier(jnp.mean(grouped * grouped, axis=2, keepdims=True)) + eps)
    normed_gate = (grouped * group_scale).reshape(ROWS, inner_width) * gate_norm_gain.astype(jnp.float32)[None, :]
    mixed_in = jnp.where(live_rows[:, None], normed_gate, 0.0).astype(jnp.bfloat16)
    output_table = jnp.transpose(adapter_output_down, (1, 0, 2)).reshape(inner_width, lane_groups)
    lane_out = jnp.dot(mixed_in, output_table, preferred_element_type=jnp.float32).reshape(ROWS, ADAPTER_COUNT, ADAPTER_RANK)
    low_out = lax.optimization_barrier(jnp.sum(lane_out * adapter_pick[:, :, None], axis=1))
    spread_output = (adapter_pick[:, :, None] * low_out[:, None, :]).reshape(ROWS, lane_groups)
    mixer_layer = jnp.dot(mixed_in, mixer_output_weight, preferred_element_type=jnp.float32)
    mixer_layer = mixer_layer + jnp.dot(spread_output, adapter_output_up.astype(jnp.float32).reshape(lane_groups, MODEL_WIDTH), precision=highest_precision)
    resid = (stream_wide + mixer_layer).astype(jnp.bfloat16)
    resid_wide = resid.astype(jnp.float32)
    mlp_scale = lax.rsqrt(lax.optimization_barrier(jnp.mean(resid_wide * resid_wide, axis=1)) + eps)
    normed_mlp = (resid_wide * mlp_scale[:, None] * mlp_norm_gain.astype(jnp.float32)[None, :]).astype(jnp.bfloat16)
    feature_block = MODEL_WIDTH // N_DP

    def add_up(block_index, running):
        first_col = block_index.astype(jnp.int32) * feature_block
        block_rows = lax.dynamic_slice_in_dim(normed_mlp, first_col, feature_block, 1)
        block_weight = lax.dynamic_slice_in_dim(mlp_up_weight, first_col, feature_block, 0)
        partial_sum = jnp.dot(block_rows, block_weight, preferred_element_type=jnp.float32).astype(jnp.bfloat16)
        partial_sum = lax.optimization_barrier(partial_sum)
        return running + partial_sum.astype(jnp.float32)
    up_sum = lax.fori_loop(0, N_DP, add_up, jnp.zeros((ROWS, FF), jnp.float32))
    hidden = (jnp.maximum(up_sum, 0.0) ** 2).astype(jnp.bfloat16)
    hidden_block = FF // N_HEAD

    def add_down(block_index, running):
        first_col = block_index.astype(jnp.int32) * hidden_block
        block_rows = lax.dynamic_slice_in_dim(hidden, first_col, hidden_block, 1)
        block_weight = lax.dynamic_slice_in_dim(mlp_down_weight, first_col, hidden_block, 0)
        partial_sum = jnp.dot(block_rows, block_weight, preferred_element_type=jnp.float32).astype(jnp.bfloat16)
        partial_sum = lax.optimization_barrier(partial_sum)
        return running + partial_sum.astype(jnp.float32)
    mlp_sum = lax.fori_loop(0, N_HEAD, add_down, jnp.zeros((ROWS, MODEL_WIDTH), jnp.float32))
    out_stream = (resid_wide + mlp_sum).astype(jnp.bfloat16)
    return (out_stream, new_state)
```

```python
import jax
import jax.numpy as jnp
from jax import lax
from jax.sharding import PartitionSpec as P

MODEL_WIDTH = 8192
HEAD_TOTAL = 128
HEAD_CHANNELS = 64
NSTATE = 128
GROUPS = 8
ADAPTER_RANK = 16
ADAPTER_COUNT = 8
TILE = 4
LANES = 128

eps = 1e-05
f32 = jnp.float32
bf16 = jnp.bfloat16


def halves(value):
    high = lax.reduce_precision(value, exponent_bits=8, mantissa_bits=7)
    return high.astype(bf16), (value - high).astype(bf16)


def split_dot(value, weight):
    high, low = halves(value)
    rows = value.shape[0]
    both = jnp.dot(jnp.concatenate([high, low], axis=0), weight, preferred_element_type=f32)
    return both[:rows] + both[rows:]


def fill(columns):
    joined = jnp.concatenate(columns, axis=1)
    return jnp.pad(joined, ((0, 0), (0, -joined.shape[1] % LANES)))


def spread_all(block, axis, count):
    copies = jnp.broadcast_to(block[None], (count,) + block.shape)
    return lax.all_to_all(copies, axis, 0, 0)


def trade(blocks, axis, groups=None):
    return lax.all_to_all(blocks, axis, 0, 0, axis_index_groups=groups)


def per_device(
    stream,
    state,
    mixer_norm_gain,
    head_input_weight,
    output_gate_weight,
    group_map_weight,
    step_size_weight,
    step_size_bias,
    head_decay_rate,
    head_skip_gain,
    gate_norm_gain,
    mixer_output_weight,
    adapter_input_down,
    adapter_input_up,
    adapter_output_down,
    adapter_output_up,
    mlp_norm_gain,
    mlp_up_weight,
    mlp_down_weight,
    slot_adapter_index,
    segment_first_slot,
):
    dp_count = lax.axis_size("dp")
    head_count = lax.axis_size("head")
    head_index = lax.axis_index("head")
    dp_index = lax.axis_index("dp")
    own_rows = state.shape[0]
    heads_here = state.shape[1]
    all_rows = own_rows * dp_count
    rows_head = all_rows // head_count
    local_width = stream.shape[1]
    inner = heads_here * HEAD_CHANNELS
    hidden_here = mlp_up_weight.shape[1]
    lane_groups = ADAPTER_COUNT * ADAPTER_RANK
    shares = head_count // GROUPS

    first_move = [(h // shares + (h % shares) * GROUPS, h) for h in range(head_count)]
    second_move = [
        (h // shares + ((h + 1) % shares) * GROUPS, h) for h in range(head_count)
    ]
    first_map = lax.ppermute(group_map_weight, "head", first_move)
    second_map = lax.ppermute(group_map_weight, "head", second_move)

    gathered = spread_all(stream, "head", head_count).reshape(all_rows, local_width)
    wide = gathered.astype(f32)
    gained = (wide * mixer_norm_gain.astype(f32)[None, :]).astype(bf16)
    mix_squares = jnp.sum(wide * wide, axis=1, keepdims=True)

    row_tile = jnp.arange(all_rows, dtype=jnp.int32) // TILE * TILE
    row_adapter = (
        jnp.sum((segment_first_slot[None, :] <= row_tile[:, None]).astype(jnp.int32), axis=1) - 1
    )
    lane_adapter = jnp.arange(lane_groups, dtype=jnp.int32) // ADAPTER_RANK
    lane_pick = row_adapter[:, None] == lane_adapter[None, :]
    input_table = jnp.transpose(adapter_input_down, (1, 0, 2)).reshape(local_width, lane_groups)
    joined = jnp.concatenate(
        [head_input_weight, output_gate_weight, first_map, second_map, input_table], axis=1
    )
    main = jnp.dot(gained, joined, preferred_element_type=f32)
    map_end = 2 * inner + 2 * NSTATE
    low = jnp.where(lane_pick, main[:, map_end:], 0.0).astype(bf16)
    step = jnp.dot(gained, step_size_weight, preferred_element_type=f32)
    step_high, step_low = halves(step)
    squares_high, squares_low = halves(mix_squares)
    sent = jnp.concatenate(
        [main[:, :map_end].astype(bf16), low, fill([step_high, step_low, squares_high, squares_low])],
        axis=1,
    )
    summed = jnp.sum(
        trade(sent.reshape(dp_count, own_rows, sent.shape[1]), "dp").astype(f32), axis=0
    )
    tail = map_end + lane_groups
    squares = summed[:, tail + 2 * heads_here : tail + 2 * heads_here + 1] + summed[
        :, tail + 2 * heads_here + 1 : tail + 2 * heads_here + 2
    ]
    mix_scale = lax.rsqrt(squares / MODEL_WIDTH + eps)
    projected = summed * mix_scale
    low_rank = projected[:, map_end:tail]
    lift = split_dot(low_rank, adapter_input_up.reshape(lane_groups, 2 * inner))
    x_part = projected[:, :inner] + lift[:, :inner]
    z_part = projected[:, inner : 2 * inner] + lift[:, inner:]
    step_raw = (
        projected[:, tail : tail + heads_here]
        + projected[:, tail + heads_here : tail + 2 * heads_here]
    )
    first_part = projected[:, 2 * inner : 2 * inner + NSTATE]
    second_part = projected[:, 2 * inner + NSTATE : map_end]
    input_first = head_index % shares == 0
    input_mat = jax.nn.silu(jnp.where(input_first, first_part, second_part))
    output_mat = jax.nn.silu(jnp.where(input_first, second_part, first_part))

    step_size = jax.nn.softplus(step_raw + step_size_bias[None, :])
    forget = jnp.exp(-step_size * head_decay_rate[None, :])
    x_heads = jax.nn.silu(x_part).reshape(own_rows, heads_here, HEAD_CHANNELS)
    old_state = state.reshape(own_rows, heads_here, HEAD_CHANNELS, NSTATE)
    fresh = (
        forget[:, :, None, None] * old_state
        + (step_size[:, :, None] * x_heads)[:, :, :, None] * input_mat[:, None, None, :]
    )
    live_rows = slot_adapter_index < ADAPTER_COUNT
    new_state = jnp.where(live_rows[:, None, None, None], fresh, old_state).reshape(state.shape)
    read_out = (
        jnp.sum(fresh * output_mat[:, None, None, :], axis=3)
        + head_skip_gain[None, :, None] * x_heads
    )
    gated = read_out.reshape(own_rows, inner) * jax.nn.silu(z_part)
    gate_squares = jnp.sum(gated * gated, axis=1, keepdims=True)
    mixed = jnp.where(
        live_rows[:, None], gated * gate_norm_gain.astype(f32)[None, :], 0.0
    ).astype(bf16)
    gate_high, gate_low = halves(gate_squares)
    mixed_all = spread_all(
        jnp.concatenate([mixed, fill([gate_high, gate_low])], axis=1), "dp", dp_count
    ).reshape(all_rows, inner + LANES)

    output_table = jnp.transpose(adapter_output_down, (1, 0, 2)).reshape(inner, lane_groups)
    joined_out = jnp.concatenate([mixer_output_weight, output_table], axis=1)
    mixed_main = jnp.dot(mixed_all[:, :inner], joined_out, preferred_element_type=f32)
    low_out = jnp.where(lane_pick, mixed_main[:, local_width:], 0.0)
    terms = mixed_main[:, :local_width] + split_dot(
        low_out, adapter_output_up.reshape(lane_groups, local_width)
    )
    mixer_sent = jnp.concatenate([terms.astype(bf16), mixed_all[:, inner:]], axis=1)
    quad = 4
    quad_groups = [list(range(q, q + quad)) for q in range(0, head_count, quad)]
    quad_rows = all_rows // quad
    parts = trade(
        mixer_sent.reshape(quad, quad_rows, mixer_sent.shape[1]), "head", quad_groups
    ).astype(f32)
    part_squares = parts[:, :, local_width : local_width + 1] + parts[
        :, :, local_width + 1 : local_width + 2
    ]
    group_squares = jnp.sum(
        part_squares.reshape(quad // shares, shares, quad_rows, 1), axis=1, keepdims=True
    )
    group_scale = lax.rsqrt(group_squares / (HEAD_TOTAL * HEAD_CHANNELS // GROUPS) + eps)
    quad_sum = jnp.sum(
        parts[:, :, :local_width].reshape(quad // shares, shares, quad_rows, local_width)
        * group_scale,
        axis=(0, 1),
    ).astype(bf16)
    mixer_all = jnp.sum(
        spread_all(quad_sum, "head", head_count)
        .astype(f32)
        .reshape(head_count // quad, quad * quad_rows, local_width),
        axis=0,
    )
    resid_all = (wide + mixer_all).astype(bf16)
    resid_wide = resid_all.astype(f32)
    mlp_squares = jnp.sum(resid_wide * resid_wide, axis=1, keepdims=True)
    mlp_in = (resid_wide * mlp_norm_gain.astype(f32)[None, :]).astype(bf16)
    resid_rows = lax.dynamic_slice_in_dim(resid_all, head_index * rows_head, rows_head, 0)
    up = jnp.dot(mlp_in, mlp_up_weight, preferred_element_type=f32).astype(bf16)
    mlp_high, mlp_low = halves(mlp_squares)
    up_sent = jnp.concatenate([up, fill([mlp_high, mlp_low])], axis=1)
    up_sum = jnp.sum(
        trade(up_sent.reshape(dp_count, own_rows, up_sent.shape[1]), "dp").astype(f32), axis=0
    )
    row_squares = (
        up_sum[:, hidden_here : hidden_here + 1] + up_sum[:, hidden_here + 1 : hidden_here + 2]
    )
    mlp_scale = lax.rsqrt(row_squares / MODEL_WIDTH + eps)
    hidden = (jnp.maximum(up_sum[:, :hidden_here] * mlp_scale, 0.0) ** 2).astype(bf16)
    hidden_all = spread_all(hidden, "dp", dp_count).reshape(all_rows, hidden_here)
    down = jnp.dot(hidden_all, mlp_down_weight, preferred_element_type=f32).astype(bf16)
    down_rows = jnp.sum(
        trade(down.reshape(head_count, rows_head, local_width), "head").astype(f32), axis=0
    )
    out_stream = (resid_rows.astype(f32) + down_rows).astype(bf16)
    return (out_stream, new_state)


def solution(mesh):
    in_specs = (
        P("head", "dp"),
        P("dp", "head", None),
        P("dp"),
        P("dp", "head"),
        P("dp", "head"),
        P("dp", "head"),
        P("dp", "head"),
        P("head"),
        P("head"),
        P("head"),
        P("head"),
        P("head", "dp"),
        P(None, "dp", None),
        P(None, None, None, "head"),
        P(None, "head", None),
        P(None, None, "dp"),
        P("dp"),
        P("dp", "head"),
        P("head", "dp"),
        P("dp"),
        P(),
    )
    out_specs = (P("head", "dp"), P("dp", "head", None))
    return jax.shard_map(
        per_device, mesh=mesh, in_specs=in_specs, out_specs=out_specs, check_vma=False
    )
```

```python
import jax
import jax.numpy as jnp
from jax import lax
from jax.sharding import PartitionSpec as P

MODEL_WIDTH = 8192
HEAD_TOTAL = 128
HEAD_CHANNELS = 64
NSTATE = 128
GROUPS = 8
ADAPTER_RANK = 16
ADAPTER_COUNT = 8
TILE = 4
LANES = 128

eps = 1e-05
f32 = jnp.float32
bf16 = jnp.bfloat16


def halves(value):
    high = lax.reduce_precision(value, exponent_bits=8, mantissa_bits=7)
    return high.astype(bf16), (value - high).astype(bf16)


def split_dot(value, weight):
    high, low = halves(value)
    rows = value.shape[0]
    both = jnp.dot(jnp.concatenate([high, low], axis=0), weight, preferred_element_type=f32)
    return both[:rows] + both[rows:]


def spread_all(block, axis, count):
    copies = jnp.broadcast_to(block[None], (count,) + block.shape)
    return lax.all_to_all(copies, axis, 0, 0)


def trade(blocks, axis, groups=None):
    return lax.all_to_all(blocks, axis, 0, 0, axis_index_groups=groups)


def per_device(
    stream,
    state,
    mixer_norm_gain,
    head_input_weight,
    output_gate_weight,
    group_map_weight,
    step_size_weight,
    step_size_bias,
    head_decay_rate,
    head_skip_gain,
    gate_norm_gain,
    mixer_output_weight,
    adapter_input_down,
    adapter_input_up,
    adapter_output_down,
    adapter_output_up,
    mlp_norm_gain,
    mlp_up_weight,
    mlp_down_weight,
    slot_adapter_index,
    segment_first_slot,
):
    dp_count = lax.axis_size("dp")
    head_count = lax.axis_size("head")
    head_index = lax.axis_index("head")
    dp_index = lax.axis_index("dp")
    own_rows = state.shape[0]
    heads_here = state.shape[1]
    all_rows = own_rows * dp_count
    rows_head = all_rows // head_count
    local_width = stream.shape[1]
    inner = heads_here * HEAD_CHANNELS
    hidden_here = mlp_up_weight.shape[1]
    lane_groups = ADAPTER_COUNT * ADAPTER_RANK
    shares = head_count // GROUPS

    first_move = [(h // shares + (h % shares) * GROUPS, h) for h in range(head_count)]
    second_move = [
        (h // shares + ((h + 1) % shares) * GROUPS, h) for h in range(head_count)
    ]
    first_map = lax.ppermute(group_map_weight, "head", first_move)
    second_map = lax.ppermute(group_map_weight, "head", second_move)

    row_tile = jnp.arange(all_rows, dtype=jnp.int32) // TILE * TILE
    row_adapter = (
        jnp.sum((segment_first_slot[None, :] <= row_tile[:, None]).astype(jnp.int32), axis=1) - 1
    )
    lane = jnp.arange(LANES, dtype=jnp.int32)
    lane_adapter = jnp.arange(lane_groups, dtype=jnp.int32) // ADAPTER_RANK
    lane_pick = (row_adapter[:, None] == lane_adapter[None, :]).astype(bf16)
    own_pick = lax.dynamic_slice_in_dim(lane_pick, dp_index * own_rows, own_rows, 0).astype(f32)
    input_table = jnp.transpose(adapter_input_down, (1, 0, 2)).reshape(local_width, lane_groups)
    joined = jnp.concatenate(
        [head_input_weight, output_gate_weight, first_map, second_map], axis=1
    )
    joined_tail = jnp.concatenate(
        [
            input_table,
            step_size_weight,
            step_size_weight,
            jnp.zeros((local_width, LANES - 2 * heads_here), bf16),
        ],
        axis=1,
    )
    at_squares = 2 * heads_here
    at_rank = at_squares + 8
    rank_here = jnp.arange(lane_groups, dtype=jnp.int32)[:, None] % ADAPTER_RANK
    fold = (rank_here + at_rank == lane[None, :]).astype(bf16)
    up_table = adapter_input_up.reshape(lane_groups, 2 * inner)
    output_table = jnp.transpose(adapter_output_down, (1, 0, 2)).reshape(inner, lane_groups)
    joined_out = jnp.concatenate([mixer_output_weight, output_table], axis=1)
    output_lift = adapter_output_up.reshape(lane_groups, local_width)
    live = jnp.broadcast_to(
        (slot_adapter_index < ADAPTER_COUNT).astype(f32)[:, None], (own_rows, LANES)
    )
    mixer_gain = mixer_norm_gain.astype(f32)[None, :]
    mlp_gain = mlp_norm_gain.astype(f32)[None, :]
    gate_gain = gate_norm_gain.astype(f32)[None, :]
    skip_gain = jnp.repeat(head_skip_gain, HEAD_CHANNELS)[None, :]
    input_first = jnp.broadcast_to((head_index % shares == 0).astype(f32), (1, LANES))
    input_second = 1.0 - input_first
    head_row = (head_index * rows_head).astype(jnp.uint32)
    pick_first = (lane[None, :] == 0).astype(f32)
    pick_second = (lane[None, :] == 1).astype(f32)
    live_inner = jnp.broadcast_to(live[:, :1], (own_rows, inner)) * gate_gain
    gathered = spread_all(stream, "head", head_count)
    (
        gathered,
        lane_pick,
        own_pick,
        joined,
        joined_tail,
        fold,
        up_table,
        joined_out,
        output_lift,
        live,
        mixer_gain,
        mlp_gain,
        skip_gain,
        input_first,
        input_second,
        head_row,
        pick_first,
        pick_second,
        live_inner,
        step_size_bias,
        head_decay_rate,
        stream,
    ) = lax.optimization_barrier(
        (
            gathered,
            lane_pick,
            own_pick,
            joined,
            joined_tail,
            fold,
            up_table,
            joined_out,
            output_lift,
            live,
            mixer_gain,
            mlp_gain,
            skip_gain,
            input_first,
            input_second,
            head_row,
            pick_first,
            pick_second,
            live_inner,
            step_size_bias,
            head_decay_rate,
            stream,
        )
    )
    wide = gathered.reshape(all_rows, local_width).astype(f32)
    gained = (wide * mixer_gain).astype(bf16)
    mix_squares = jnp.sum(wide * wide, axis=1, keepdims=True)
    main = jnp.dot(gained, joined, preferred_element_type=f32).astype(bf16)
    tail = jnp.dot(gained, joined_tail, preferred_element_type=f32)
    low = jnp.dot(tail[:, :lane_groups].astype(bf16) * lane_pick, fold, preferred_element_type=f32)
    step = tail[:, lane_groups:]
    column = lane[None, :]
    wanted = jnp.where(column < at_squares, step, mix_squares)
    high = lax.reduce_precision(wanted, exponent_bits=8, mantissa_bits=7)
    is_high = (column < heads_here) | (column == at_squares)
    exact = jnp.where(is_high, high, wanted - high)
    last = jnp.where(column < at_rank, exact, low).astype(bf16)
    sent = jnp.concatenate([main, last], axis=1)
    summed = jnp.sum(
        trade(sent.reshape(dp_count, own_rows, sent.shape[1]), "dp").astype(f32), axis=0
    )
    map_end = 2 * inner + 2 * NSTATE
    last = summed[:, map_end:]
    squares = last[:, at_squares : at_squares + 1] + last[:, at_squares + 1 : at_squares + 2]
    mix_scale = lax.rsqrt(squares / MODEL_WIDTH + eps)
    projected = summed * mix_scale
    last = last * mix_scale
    low_rank = last[:, at_rank : at_rank + ADAPTER_RANK]
    spread_low = jnp.concatenate([low_rank] * ADAPTER_COUNT, axis=1) * own_pick
    lift = split_dot(spread_low, up_table)
    x_part = projected[:, :inner] + lift[:, :inner]
    z_part = projected[:, inner : 2 * inner] + lift[:, inner:]
    step_raw = last[:, :heads_here] + last[:, heads_here : 2 * heads_here]
    first_part = projected[:, 2 * inner : 2 * inner + NSTATE]
    second_part = projected[:, 2 * inner + NSTATE : map_end]
    input_mat = jax.nn.silu(first_part * input_first + second_part * input_second)
    output_mat = jax.nn.silu(second_part * input_first + first_part * input_second)

    step_size = jax.nn.softplus(step_raw + step_size_bias[None, :])
    forget = jnp.exp(-step_size * head_decay_rate[None, :])
    x_heads = jax.nn.silu(x_part).reshape(own_rows, heads_here, HEAD_CHANNELS)
    old_state = state.reshape(own_rows, heads_here, HEAD_CHANNELS, NSTATE)
    step_x = step_size[:, :, None] * x_heads
    fresh = (
        forget[:, :, None, None] * old_state + step_x[:, :, :, None] * input_mat[:, None, None, :]
    )
    read_out = (
        jnp.sum(fresh * output_mat[:, None, None, :], axis=3).reshape(own_rows, inner)
        + skip_gain * x_heads.reshape(own_rows, inner)
    )
    gated = read_out * jax.nn.silu(z_part)
    gate_squares = jnp.sum(gated * gated, axis=1, keepdims=True)
    mixed = (gated * live_inner).astype(bf16)
    gate_high = lax.reduce_precision(gate_squares, exponent_bits=8, mantissa_bits=7)
    gate_tail = (gate_high * pick_first + (gate_squares - gate_high) * pick_second).astype(bf16)
    mixed_all = spread_all(
        jnp.concatenate([mixed, gate_tail], axis=1), "dp", dp_count
    ).reshape(all_rows, inner + LANES)

    mixed_main = jnp.dot(mixed_all[:, :inner], joined_out, preferred_element_type=f32)
    low_out = mixed_main[:, local_width:] * lane_pick.astype(f32)
    terms = mixed_main[:, :local_width] + split_dot(low_out, output_lift)
    mixer_sent = jnp.concatenate([terms.astype(bf16), mixed_all[:, inner:]], axis=1)
    quad = 4
    quad_groups = [list(range(q, q + quad)) for q in range(0, head_count, quad)]
    quad_rows = all_rows // quad
    parts = trade(
        mixer_sent.reshape(quad, quad_rows, mixer_sent.shape[1]), "head", quad_groups
    ).astype(f32)
    part_squares = parts[:, :, local_width : local_width + 1] + parts[
        :, :, local_width + 1 : local_width + 2
    ]
    group_squares = jnp.sum(
        part_squares.reshape(quad // shares, shares, quad_rows, 1), axis=1, keepdims=True
    )
    group_scale = lax.rsqrt(group_squares / (HEAD_TOTAL * HEAD_CHANNELS // GROUPS) + eps)
    quad_sum = jnp.sum(
        parts[:, :, :local_width].reshape(quad // shares, shares, quad_rows, local_width)
        * group_scale,
        axis=(0, 1),
    ).astype(bf16)
    mixer_all = jnp.sum(
        spread_all(quad_sum, "head", head_count)
        .astype(f32)
        .reshape(head_count // quad, quad * quad_rows, local_width),
        axis=0,
    )
    resid_all = (wide + mixer_all).astype(bf16)
    resid_wide = resid_all.astype(f32)
    mlp_squares = jnp.sum(resid_wide * resid_wide, axis=1, keepdims=True)
    mlp_in = (resid_wide * mlp_gain).astype(bf16)
    up = jnp.dot(mlp_in, mlp_up_weight, preferred_element_type=f32).astype(bf16)
    mlp_high = lax.reduce_precision(mlp_squares, exponent_bits=8, mantissa_bits=7)
    up_tail = (mlp_high * pick_first + (mlp_squares - mlp_high) * pick_second).astype(bf16)
    up_sent = jnp.concatenate([up, up_tail], axis=1)
    resid_rows = lax.dynamic_slice_in_dim(resid_all, head_row, rows_head, 0)
    up_sent, resid_rows = lax.optimization_barrier((up_sent, resid_rows))
    up_sum = jnp.sum(
        trade(up_sent.reshape(dp_count, own_rows, up_sent.shape[1]), "dp").astype(f32), axis=0
    )
    row_squares = (
        up_sum[:, hidden_here : hidden_here + 1] + up_sum[:, hidden_here + 1 : hidden_here + 2]
    )
    mlp_scale = lax.rsqrt(row_squares / MODEL_WIDTH + eps)
    hidden = (jnp.maximum(up_sum[:, :hidden_here] * mlp_scale, 0.0) ** 2).astype(bf16)
    hidden_all = spread_all(hidden, "dp", dp_count).reshape(all_rows, hidden_here)
    down = jnp.dot(hidden_all, mlp_down_weight, preferred_element_type=f32).astype(bf16)
    down, old_state, live, forget, step_x, input_mat = lax.optimization_barrier(
        (down, old_state, live, forget, step_x, input_mat)
    )
    fresh = (
        forget[:, :, None, None] * old_state + step_x[:, :, :, None] * input_mat[:, None, None, :]
    )
    new_state = jnp.where(live[:, 0, None, None, None] > 0, fresh, old_state).reshape(state.shape)
    down_rows = jnp.sum(
        trade(down.reshape(head_count, rows_head, local_width), "head").astype(f32), axis=0
    )
    out_stream = (resid_rows.astype(f32) + down_rows).astype(bf16)
    return (out_stream, new_state)


def solution(mesh):
    in_specs = (
        P("head", "dp"),
        P("dp", "head", None),
        P("dp"),
        P("dp", "head"),
        P("dp", "head"),
        P("dp", "head"),
        P("dp", "head"),
        P("head"),
        P("head"),
        P("head"),
        P("head"),
        P("head", "dp"),
        P(None, "dp", None),
        P(None, None, None, "head"),
        P(None, "head", None),
        P(None, None, "dp"),
        P("dp"),
        P("dp", "head"),
        P("head", "dp"),
        P("dp"),
        P(),
    )
    out_specs = (P("head", "dp"), P("dp", "head", None))
    return jax.shard_map(
        per_device, mesh=mesh, in_specs=in_specs, out_specs=out_specs, check_vma=False
    )
```

```python
import jax
import jax.numpy as jnp
from jax import lax
from jax.sharding import PartitionSpec as P

MODEL_WIDTH = 8192
HEAD_TOTAL = 128
HEAD_CHANNELS = 64
NSTATE = 128
GROUPS = 8
ADAPTER_RANK = 16
ADAPTER_COUNT = 8
TILE = 4
LANES = 128

eps = 1e-05
f32 = jnp.float32
bf16 = jnp.bfloat16


def halves(value):
    high = lax.reduce_precision(value, exponent_bits=8, mantissa_bits=7)
    return high.astype(bf16), (value - high).astype(bf16)


def split_dot(value, weight):
    high, low = halves(value)
    rows = value.shape[0]
    both = jnp.dot(jnp.concatenate([high, low], axis=0), weight, preferred_element_type=f32)
    return both[:rows] + both[rows:]


def spread_all(block, axis, count):
    copies = jnp.broadcast_to(block[None], (count,) + block.shape)
    return lax.all_to_all(copies, axis, 0, 0)


def trade(blocks, axis, groups=None):
    return lax.all_to_all(blocks, axis, 0, 0, axis_index_groups=groups)


def per_device(
    stream,
    state,
    mixer_norm_gain,
    head_input_weight,
    output_gate_weight,
    group_map_weight,
    step_size_weight,
    step_size_bias,
    head_decay_rate,
    head_skip_gain,
    gate_norm_gain,
    mixer_output_weight,
    adapter_input_down,
    adapter_input_up,
    adapter_output_down,
    adapter_output_up,
    mlp_norm_gain,
    mlp_up_weight,
    mlp_down_weight,
    slot_adapter_index,
    segment_first_slot,
):
    dp_count = lax.axis_size("dp")
    head_count = lax.axis_size("head")
    head_index = lax.axis_index("head")
    dp_index = lax.axis_index("dp")
    own_rows = state.shape[0]
    heads_here = state.shape[1]
    all_rows = own_rows * dp_count
    rows_head = all_rows // head_count
    local_width = stream.shape[1]
    inner = heads_here * HEAD_CHANNELS
    hidden_here = mlp_up_weight.shape[1]
    lane_groups = ADAPTER_COUNT * ADAPTER_RANK
    shares = head_count // GROUPS

    first_move = [(h // shares + (h % shares) * GROUPS, h) for h in range(head_count)]
    second_move = [
        (h // shares + ((h + 1) % shares) * GROUPS, h) for h in range(head_count)
    ]
    first_map = lax.ppermute(group_map_weight, "head", first_move)
    second_map = lax.ppermute(group_map_weight, "head", second_move)

    row_tile = jnp.arange(all_rows, dtype=jnp.int32) // TILE * TILE
    row_adapter = (
        jnp.sum((segment_first_slot[None, :] <= row_tile[:, None]).astype(jnp.int32), axis=1) - 1
    )
    lane = jnp.arange(LANES, dtype=jnp.int32)
    lane_adapter = jnp.arange(lane_groups, dtype=jnp.int32) // ADAPTER_RANK
    lane_pick = (row_adapter[:, None] == lane_adapter[None, :]).astype(bf16)
    own_pick = lax.dynamic_slice_in_dim(lane_pick, dp_index * own_rows, own_rows, 0).astype(f32)
    input_table = jnp.transpose(adapter_input_down, (1, 0, 2)).reshape(local_width, lane_groups)
    joined = jnp.concatenate(
        [head_input_weight, output_gate_weight, first_map, second_map], axis=1
    )
    joined_tail = jnp.concatenate(
        [
            input_table,
            step_size_weight,
            step_size_weight,
            jnp.zeros((local_width, LANES - 2 * heads_here), bf16),
        ],
        axis=1,
    )
    at_squares = 2 * heads_here
    at_rank = at_squares + 8
    rank_here = jnp.arange(lane_groups, dtype=jnp.int32)[:, None] % ADAPTER_RANK
    fold = (rank_here + at_rank == lane[None, :]).astype(bf16)
    up_table = adapter_input_up.reshape(lane_groups, 2 * inner)
    output_table = jnp.transpose(adapter_output_down, (1, 0, 2)).reshape(inner, lane_groups)
    joined_out = jnp.concatenate([mixer_output_weight, output_table], axis=1)
    output_lift = adapter_output_up.reshape(lane_groups, local_width)
    live = jnp.broadcast_to(
        (slot_adapter_index < ADAPTER_COUNT).astype(f32)[:, None], (own_rows, LANES)
    )
    mixer_gain = mixer_norm_gain.astype(f32)[None, :]
    mlp_gain = mlp_norm_gain.astype(f32)[None, :]
    gate_gain = gate_norm_gain.astype(f32)[None, :]
    skip_gain = jnp.repeat(head_skip_gain, HEAD_CHANNELS)[None, :]
    input_first = jnp.broadcast_to((head_index % shares == 0).astype(f32), (1, LANES))
    input_second = 1.0 - input_first
    head_row = (head_index * rows_head).astype(jnp.uint32)
    pick_first = (lane[None, :] == 0).astype(f32)
    pick_second = (lane[None, :] == 1).astype(f32)
    live_inner = jnp.broadcast_to(live[:, :1], (own_rows, inner)) * gate_gain
    gathered = spread_all(stream, "head", head_count)
    (
        gathered,
        lane_pick,
        own_pick,
        joined,
        joined_tail,
        fold,
        up_table,
        joined_out,
        output_lift,
        live,
        mixer_gain,
        mlp_gain,
        skip_gain,
        input_first,
        input_second,
        head_row,
        pick_first,
        pick_second,
        live_inner,
        step_size_bias,
        head_decay_rate,
        stream,
    ) = lax.optimization_barrier(
        (
            gathered,
            lane_pick,
            own_pick,
            joined,
            joined_tail,
            fold,
            up_table,
            joined_out,
            output_lift,
            live,
            mixer_gain,
            mlp_gain,
            skip_gain,
            input_first,
            input_second,
            head_row,
            pick_first,
            pick_second,
            live_inner,
            step_size_bias,
            head_decay_rate,
            stream,
        )
    )
    wide = gathered.reshape(all_rows, local_width).astype(f32)
    gained = (wide * mixer_gain).astype(bf16)
    mix_squares = jnp.sum(wide * wide, axis=1, keepdims=True)
    main = jnp.dot(gained, joined, preferred_element_type=f32).astype(bf16)
    tail = jnp.dot(gained, joined_tail, preferred_element_type=f32)
    low = jnp.dot(tail[:, :lane_groups].astype(bf16) * lane_pick, fold, preferred_element_type=f32)
    step = tail[:, lane_groups:]
    column = lane[None, :]
    wanted = jnp.where(column < at_squares, step, mix_squares)
    high = lax.reduce_precision(wanted, exponent_bits=8, mantissa_bits=7)
    is_high = (column < heads_here) | (column == at_squares)
    exact = jnp.where(is_high, high, wanted - high)
    last = jnp.where(column < at_rank, exact, low).astype(bf16)
    sent = jnp.concatenate([main, last], axis=1)
    summed = jnp.sum(
        trade(sent.reshape(dp_count, own_rows, sent.shape[1]), "dp").astype(f32), axis=0
    )
    map_end = 2 * inner + 2 * NSTATE
    last = summed[:, map_end:]
    squares = last[:, at_squares : at_squares + 1] + last[:, at_squares + 1 : at_squares + 2]
    mix_scale = lax.rsqrt(squares / MODEL_WIDTH + eps)
    projected = summed * mix_scale
    last = last * mix_scale
    low_rank = last[:, at_rank : at_rank + ADAPTER_RANK]
    spread_low = jnp.concatenate([low_rank] * ADAPTER_COUNT, axis=1) * own_pick
    lift = split_dot(spread_low, up_table)
    x_part = projected[:, :inner] + lift[:, :inner]
    z_part = projected[:, inner : 2 * inner] + lift[:, inner:]
    step_raw = last[:, :heads_here] + last[:, heads_here : 2 * heads_here]
    first_part = projected[:, 2 * inner : 2 * inner + NSTATE]
    second_part = projected[:, 2 * inner + NSTATE : map_end]
    input_mat = jax.nn.silu(first_part * input_first + second_part * input_second)
    output_mat = jax.nn.silu(second_part * input_first + first_part * input_second)

    step_size = jax.nn.softplus(step_raw + step_size_bias[None, :])
    forget = jnp.exp(-step_size * head_decay_rate[None, :])
    x_heads = jax.nn.silu(x_part).reshape(own_rows, heads_here, HEAD_CHANNELS)
    old_state = state.reshape(own_rows, heads_here, HEAD_CHANNELS, NSTATE)
    step_x = step_size[:, :, None] * x_heads
    maps_product = jnp.sum(input_mat * output_mat, axis=1)[:, None, None]
    read_heads = (
        forget[:, :, None] * jnp.sum(old_state * output_mat[:, None, None, :], axis=3)
        + step_x * maps_product
    )
    read_out = read_heads.reshape(own_rows, inner) + skip_gain * x_heads.reshape(
        own_rows, inner
    )
    gated = read_out * jax.nn.silu(z_part)
    gate_squares = jnp.sum(gated * gated, axis=1, keepdims=True)
    mixed = (gated * live_inner).astype(bf16)
    gate_high = lax.reduce_precision(gate_squares, exponent_bits=8, mantissa_bits=7)
    gate_tail = (gate_high * pick_first + (gate_squares - gate_high) * pick_second).astype(bf16)
    mixed_all = spread_all(
        jnp.concatenate([mixed, gate_tail], axis=1), "dp", dp_count
    ).reshape(all_rows, inner + LANES)

    mixed_main = jnp.dot(mixed_all[:, :inner], joined_out, preferred_element_type=f32)
    low_out = mixed_main[:, local_width:] * lane_pick.astype(f32)
    terms = mixed_main[:, :local_width] + split_dot(low_out, output_lift)
    mixer_sent = jnp.concatenate([terms.astype(bf16), mixed_all[:, inner:]], axis=1)
    quad = 4
    quad_groups = [list(range(q, q + quad)) for q in range(0, head_count, quad)]
    quad_rows = all_rows // quad
    parts = trade(
        mixer_sent.reshape(quad, quad_rows, mixer_sent.shape[1]), "head", quad_groups
    ).astype(f32)
    part_squares = parts[:, :, local_width : local_width + 1] + parts[
        :, :, local_width + 1 : local_width + 2
    ]
    group_squares = jnp.sum(
        part_squares.reshape(quad // shares, shares, quad_rows, 1), axis=1, keepdims=True
    )
    group_scale = lax.rsqrt(group_squares / (HEAD_TOTAL * HEAD_CHANNELS // GROUPS) + eps)
    quad_sum = jnp.sum(
        parts[:, :, :local_width].reshape(quad // shares, shares, quad_rows, local_width)
        * group_scale,
        axis=(0, 1),
    ).astype(bf16)
    mixer_all = jnp.sum(
        spread_all(quad_sum, "head", head_count)
        .astype(f32)
        .reshape(head_count // quad, quad * quad_rows, local_width),
        axis=0,
    )
    resid_all = (wide + mixer_all).astype(bf16)
    resid_wide = resid_all.astype(f32)
    mlp_squares = jnp.sum(resid_wide * resid_wide, axis=1, keepdims=True)
    mlp_in = (resid_wide * mlp_gain).astype(bf16)
    up = jnp.dot(mlp_in, mlp_up_weight, preferred_element_type=f32).astype(bf16)
    mlp_high = lax.reduce_precision(mlp_squares, exponent_bits=8, mantissa_bits=7)
    up_tail = (mlp_high * pick_first + (mlp_squares - mlp_high) * pick_second).astype(bf16)
    up_sent = jnp.concatenate([up, up_tail], axis=1)
    resid_rows = lax.dynamic_slice_in_dim(resid_all, head_row, rows_head, 0)
    up_sent, resid_rows = lax.optimization_barrier((up_sent, resid_rows))
    up_sum = jnp.sum(
        trade(up_sent.reshape(dp_count, own_rows, up_sent.shape[1]), "dp").astype(f32), axis=0
    )
    row_squares = (
        up_sum[:, hidden_here : hidden_here + 1] + up_sum[:, hidden_here + 1 : hidden_here + 2]
    )
    mlp_scale = lax.rsqrt(row_squares / MODEL_WIDTH + eps)
    hidden = (jnp.maximum(up_sum[:, :hidden_here] * mlp_scale, 0.0) ** 2).astype(bf16)
    hidden_all = spread_all(hidden, "dp", dp_count).reshape(all_rows, hidden_here)
    down = jnp.dot(hidden_all, mlp_down_weight, preferred_element_type=f32).astype(bf16)
    down, old_state, live, forget, step_x, input_mat = lax.optimization_barrier(
        (down, old_state, live, forget, step_x, input_mat)
    )
    fresh = (
        forget[:, :, None, None] * old_state + step_x[:, :, :, None] * input_mat[:, None, None, :]
    )
    new_state = jnp.where(live[:, 0, None, None, None] > 0, fresh, old_state).reshape(state.shape)
    down_rows = jnp.sum(
        trade(down.reshape(head_count, rows_head, local_width), "head").astype(f32), axis=0
    )
    out_stream = (resid_rows.astype(f32) + down_rows).astype(bf16)
    return (out_stream, new_state)


def solution(mesh):
    in_specs = (
        P("head", "dp"),
        P("dp", "head", None),
        P("dp"),
        P("dp", "head"),
        P("dp", "head"),
        P("dp", "head"),
        P("dp", "head"),
        P("head"),
        P("head"),
        P("head"),
        P("head"),
        P("head", "dp"),
        P(None, "dp", None),
        P(None, None, None, "head"),
        P(None, "head", None),
        P(None, None, "dp"),
        P("dp"),
        P("dp", "head"),
        P("head", "dp"),
        P("dp"),
        P(),
    )
    out_specs = (P("head", "dp"), P("dp", "head", None))
    return jax.shard_map(
        per_device, mesh=mesh, in_specs=in_specs, out_specs=out_specs, check_vma=False
    )
```

```python
import jax
import jax.numpy as jnp
from jax import lax
from jax.sharding import PartitionSpec as P

MODEL_WIDTH = 8192
HEAD_TOTAL = 128
HEAD_CHANNELS = 64
NSTATE = 128
GROUPS = 8
ADAPTER_RANK = 16
ADAPTER_COUNT = 8
TILE = 4
LANES = 128

eps = 1e-05
f32 = jnp.float32
bf16 = jnp.bfloat16


def halves(value):
    high = lax.reduce_precision(value, exponent_bits=8, mantissa_bits=7)
    return high.astype(bf16), (value - high).astype(bf16)


def split_dot(value, weight):
    high, low = halves(value)
    rows = value.shape[0]
    both = jnp.dot(jnp.concatenate([high, low], axis=0), weight, preferred_element_type=f32)
    return both[:rows] + both[rows:]


def spread_all(block, axis, count):
    copies = jnp.broadcast_to(block[None], (count,) + block.shape)
    return lax.all_to_all(copies, axis, 0, 0)


def trade(blocks, axis, groups=None):
    return lax.all_to_all(blocks, axis, 0, 0, axis_index_groups=groups)


def per_device(
    stream,
    state,
    mixer_norm_gain,
    head_input_weight,
    output_gate_weight,
    group_map_weight,
    step_size_weight,
    step_size_bias,
    head_decay_rate,
    head_skip_gain,
    gate_norm_gain,
    mixer_output_weight,
    adapter_input_down,
    adapter_input_up,
    adapter_output_down,
    adapter_output_up,
    mlp_norm_gain,
    mlp_up_weight,
    mlp_down_weight,
    slot_adapter_index,
    segment_first_slot,
):
    dp_count = lax.axis_size("dp")
    head_count = lax.axis_size("head")
    head_index = lax.axis_index("head")
    dp_index = lax.axis_index("dp")
    own_rows = state.shape[0]
    heads_here = state.shape[1]
    all_rows = own_rows * dp_count
    rows_head = all_rows // head_count
    local_width = stream.shape[1]
    inner = heads_here * HEAD_CHANNELS
    hidden_here = mlp_up_weight.shape[1]
    lane_groups = ADAPTER_COUNT * ADAPTER_RANK
    shares = head_count // GROUPS

    first_move = [(h // shares + (h % shares) * GROUPS, h) for h in range(head_count)]
    second_move = [
        (h // shares + ((h + 1) % shares) * GROUPS, h) for h in range(head_count)
    ]
    first_map = lax.ppermute(group_map_weight, "head", first_move)
    second_map = lax.ppermute(group_map_weight, "head", second_move)

    row_tile = jnp.arange(all_rows, dtype=jnp.int32) // TILE * TILE
    row_adapter = (
        jnp.sum((segment_first_slot[None, :] <= row_tile[:, None]).astype(jnp.int32), axis=1) - 1
    )
    lane = jnp.arange(LANES, dtype=jnp.int32)
    lane_adapter = jnp.arange(lane_groups, dtype=jnp.int32) // ADAPTER_RANK
    lane_pick = (row_adapter[:, None] == lane_adapter[None, :]).astype(bf16)
    own_pick = lax.dynamic_slice_in_dim(lane_pick, dp_index * own_rows, own_rows, 0).astype(f32)
    input_table = jnp.transpose(adapter_input_down, (1, 0, 2)).reshape(local_width, lane_groups)
    joined = jnp.concatenate(
        [head_input_weight, output_gate_weight, first_map, second_map], axis=1
    )
    joined_tail = jnp.concatenate(
        [
            input_table,
            step_size_weight,
            step_size_weight,
            jnp.zeros((local_width, LANES - 2 * heads_here), bf16),
        ],
        axis=1,
    )
    at_squares = 2 * heads_here
    at_rank = at_squares + 8
    rank_here = jnp.arange(lane_groups, dtype=jnp.int32)[:, None] % ADAPTER_RANK
    fold = (rank_here + at_rank == lane[None, :]).astype(bf16)
    up_table = adapter_input_up.reshape(lane_groups, 2 * inner)
    output_table = jnp.transpose(adapter_output_down, (1, 0, 2)).reshape(inner, lane_groups)
    joined_out = jnp.concatenate([mixer_output_weight, output_table], axis=1)
    output_lift = adapter_output_up.reshape(lane_groups, local_width)
    live = jnp.broadcast_to(
        (slot_adapter_index < ADAPTER_COUNT).astype(f32)[:, None], (own_rows, LANES)
    )
    mixer_gain = mixer_norm_gain.astype(f32)[None, :]
    mlp_gain = mlp_norm_gain.astype(f32)[None, :]
    gate_gain = gate_norm_gain.astype(f32)[None, :]
    skip_gain = jnp.repeat(head_skip_gain, HEAD_CHANNELS)[None, :]
    input_first = jnp.broadcast_to((head_index % shares == 0).astype(f32), (1, LANES))
    input_second = 1.0 - input_first
    head_row = (head_index * rows_head).astype(jnp.uint32)
    pick_first = (lane[None, :] == 0).astype(f32)
    pick_second = (lane[None, :] == 1).astype(f32)
    live_inner = jnp.broadcast_to(live[:, :1], (own_rows, inner)) * gate_gain
    gathered = spread_all(stream, "head", head_count)
    (
        gathered,
        lane_pick,
        own_pick,
        joined,
        joined_tail,
        fold,
        up_table,
        joined_out,
        output_lift,
        live,
        mixer_gain,
        mlp_gain,
        skip_gain,
        input_first,
        input_second,
        head_row,
        pick_first,
        pick_second,
        live_inner,
        step_size_bias,
        head_decay_rate,
        stream,
    ) = lax.optimization_barrier(
        (
            gathered,
            lane_pick,
            own_pick,
            joined,
            joined_tail,
            fold,
            up_table,
            joined_out,
            output_lift,
            live,
            mixer_gain,
            mlp_gain,
            skip_gain,
            input_first,
            input_second,
            head_row,
            pick_first,
            pick_second,
            live_inner,
            step_size_bias,
            head_decay_rate,
            stream,
        )
    )
    wide = gathered.reshape(all_rows, local_width).astype(f32)
    gained = (wide * mixer_gain).astype(bf16)
    mix_squares = jnp.sum(wide * wide, axis=1, keepdims=True)
    main = jnp.dot(gained, joined, preferred_element_type=f32).astype(bf16)
    tail = jnp.dot(gained, joined_tail, preferred_element_type=f32)
    low = jnp.dot(tail[:, :lane_groups].astype(bf16) * lane_pick, fold, preferred_element_type=f32)
    step = tail[:, lane_groups:]
    column = lane[None, :]
    wanted = jnp.where(column < at_squares, step, mix_squares)
    high = lax.reduce_precision(wanted, exponent_bits=8, mantissa_bits=7)
    is_high = (column < heads_here) | (column == at_squares)
    exact = jnp.where(is_high, high, wanted - high)
    last = jnp.where(column < at_rank, exact, low).astype(bf16)
    sent = jnp.concatenate([main, last], axis=1)
    summed = jnp.sum(
        trade(sent.reshape(dp_count, own_rows, sent.shape[1]), "dp").astype(f32), axis=0
    )
    map_end = 2 * inner + 2 * NSTATE
    last = summed[:, map_end:]
    squares = last[:, at_squares : at_squares + 1] + last[:, at_squares + 1 : at_squares + 2]
    mix_scale = lax.rsqrt(squares / MODEL_WIDTH + eps)
    projected = summed * mix_scale
    last = last * mix_scale
    low_rank = last[:, at_rank : at_rank + ADAPTER_RANK]
    spread_low = jnp.concatenate([low_rank] * ADAPTER_COUNT, axis=1) * own_pick
    lift = split_dot(spread_low, up_table)
    x_part = projected[:, :inner] + lift[:, :inner]
    z_part = projected[:, inner : 2 * inner] + lift[:, inner:]
    step_raw = last[:, :heads_here] + last[:, heads_here : 2 * heads_here]
    first_part = projected[:, 2 * inner : 2 * inner + NSTATE]
    second_part = projected[:, 2 * inner + NSTATE : map_end]
    input_mat = jax.nn.silu(first_part * input_first + second_part * input_second)
    output_mat = jax.nn.silu(second_part * input_first + first_part * input_second)

    step_size = jax.nn.softplus(step_raw + step_size_bias[None, :])
    forget = jnp.exp(-step_size * head_decay_rate[None, :])
    x_heads = jax.nn.silu(x_part).reshape(own_rows, heads_here, HEAD_CHANNELS)
    old_state = state.reshape(own_rows, heads_here, HEAD_CHANNELS, NSTATE)
    step_x = step_size[:, :, None] * x_heads
    maps_product = jnp.sum(input_mat * output_mat, axis=1)[:, None, None]
    read_heads = (
        forget[:, :, None] * jnp.sum(old_state * output_mat[:, None, None, :], axis=3)
        + step_x * maps_product
    )
    read_out = read_heads.reshape(own_rows, inner) + skip_gain * x_heads.reshape(
        own_rows, inner
    )
    gated = read_out * jax.nn.silu(z_part)
    gate_squares = jnp.sum(gated * gated, axis=1, keepdims=True)
    mixed = (gated * live_inner).astype(bf16)
    gate_high = lax.reduce_precision(gate_squares, exponent_bits=8, mantissa_bits=7)
    gate_tail = (gate_high * pick_first + (gate_squares - gate_high) * pick_second).astype(bf16)
    mixed_sent, forget, step_x, input_mat = lax.optimization_barrier(
        (jnp.concatenate([mixed, gate_tail], axis=1), forget, step_x, input_mat)
    )
    mixed_all = spread_all(mixed_sent, "dp", dp_count).reshape(all_rows, inner + LANES)

    mixed_main = jnp.dot(mixed_all[:, :inner], joined_out, preferred_element_type=f32)
    low_out = mixed_main[:, local_width:] * lane_pick.astype(f32)
    terms = mixed_main[:, :local_width] + split_dot(low_out, output_lift)
    mixer_sent = jnp.concatenate([terms.astype(bf16), mixed_all[:, inner:]], axis=1)
    quad = 4
    quad_groups = [list(range(q, q + quad)) for q in range(0, head_count, quad)]
    quad_rows = all_rows // quad
    parts = trade(
        mixer_sent.reshape(quad, quad_rows, mixer_sent.shape[1]), "head", quad_groups
    ).astype(f32)
    part_squares = parts[:, :, local_width : local_width + 1] + parts[
        :, :, local_width + 1 : local_width + 2
    ]
    group_squares = jnp.sum(
        part_squares.reshape(quad // shares, shares, quad_rows, 1), axis=1, keepdims=True
    )
    group_scale = lax.rsqrt(group_squares / (HEAD_TOTAL * HEAD_CHANNELS // GROUPS) + eps)
    quad_sum = jnp.sum(
        parts[:, :, :local_width].reshape(quad // shares, shares, quad_rows, local_width)
        * group_scale,
        axis=(0, 1),
    ).astype(bf16)
    mixer_all = jnp.sum(
        spread_all(quad_sum, "head", head_count)
        .astype(f32)
        .reshape(head_count // quad, quad * quad_rows, local_width),
        axis=0,
    )
    resid_all = (wide + mixer_all).astype(bf16)
    resid_wide = resid_all.astype(f32)
    mlp_squares = jnp.sum(resid_wide * resid_wide, axis=1, keepdims=True)
    mlp_in = (resid_wide * mlp_gain).astype(bf16)
    up = jnp.dot(mlp_in, mlp_up_weight, preferred_element_type=f32).astype(bf16)
    mlp_high = lax.reduce_precision(mlp_squares, exponent_bits=8, mantissa_bits=7)
    up_tail = (mlp_high * pick_first + (mlp_squares - mlp_high) * pick_second).astype(bf16)
    up_sent = jnp.concatenate([up, up_tail], axis=1)
    resid_rows = lax.dynamic_slice_in_dim(resid_all, head_row, rows_head, 0)
    up_sent, resid_rows = lax.optimization_barrier((up_sent, resid_rows))
    up_sum = jnp.sum(
        trade(up_sent.reshape(dp_count, own_rows, up_sent.shape[1]), "dp").astype(f32), axis=0
    )
    row_squares = (
        up_sum[:, hidden_here : hidden_here + 1] + up_sum[:, hidden_here + 1 : hidden_here + 2]
    )
    mlp_scale = lax.rsqrt(row_squares / MODEL_WIDTH + eps)
    hidden = (jnp.maximum(up_sum[:, :hidden_here] * mlp_scale, 0.0) ** 2).astype(bf16)
    hidden_all = spread_all(hidden, "dp", dp_count).reshape(all_rows, hidden_here)
    down = jnp.dot(hidden_all, mlp_down_weight, preferred_element_type=f32).astype(bf16)
    down, old_state, live, forget, step_x, input_mat = lax.optimization_barrier(
        (down, old_state, live, forget, step_x, input_mat)
    )
    fresh = (
        forget[:, :, None, None] * old_state + step_x[:, :, :, None] * input_mat[:, None, None, :]
    )
    new_state = jnp.where(live[:, 0, None, None, None] > 0, fresh, old_state).reshape(state.shape)
    down_rows = jnp.sum(
        trade(down.reshape(head_count, rows_head, local_width), "head").astype(f32), axis=0
    )
    out_stream = (resid_rows.astype(f32) + down_rows).astype(bf16)
    return (out_stream, new_state)


def solution(mesh):
    in_specs = (
        P("head", "dp"),
        P("dp", "head", None),
        P("dp"),
        P("dp", "head"),
        P("dp", "head"),
        P("dp", "head"),
        P("dp", "head"),
        P("head"),
        P("head"),
        P("head"),
        P("head"),
        P("head", "dp"),
        P(None, "dp", None),
        P(None, None, None, "head"),
        P(None, "head", None),
        P(None, None, "dp"),
        P("dp"),
        P("dp", "head"),
        P("head", "dp"),
        P("dp"),
        P(),
    )
    out_specs = (P("head", "dp"), P("dp", "head", None))
    return jax.shard_map(
        per_device, mesh=mesh, in_specs=in_specs, out_specs=out_specs, check_vma=False
    )
```
